128 devices in a mesh: lat: 32 (over z, y, core), wave: 4 (over x).
Axes of the slice: x: 4, y: 4, z: 4, core: 2. Of those that a mesh axis runs over, the one named last changes fastest.
Arguments:
- spectra: float32 [1280, 2, 128, 640], P(('lat', 'wave')), may hold values from -0.01171875 to 0.01171875
- legendre: float32 [128, 1280, 2, 640], P(None, ('lat', 'wave')), may hold values from -4 to 4
- weights: float32 [128], replicated, may hold values from 1 to 4
- counts: int32 [128], P('lat'), may hold values from 5116 to 5632, as said below
- assign: int32 [1280], replicated, may hold values from 0 to 1279, as said below
Outputs:
- harmonic_products: float32 [1280, 2, 128, 640], P(('lat', 'wave'))
The draws below stay inside these ranges and needn't reach their ends.
Inputs may be any that keep to these rules, and one draw needn't show every extreme that they name: `counts`: pair j has 5632 - 4 (127 - j) - 4 r points with r one of 0, 1, 2; the pair nearest the equator, j = 127, has exactly 5632. `assign`: A permutation of 0 to 1279 in which slots 2 s and 2 s + 1 hold a wavenumber m and 1279 - m.
All inputs are finite; a program needn't handle non-finite values.
Results may differ from the reference program's by a relative error of at most 0.0003.
Values sent between devices are 32-bit elements; how exact they have to be, the bound alone decides.
A program may use at most 128 MiB of HBM per device.

```python
import math
import jax
import jax.numpy as jnp
from jax import lax

M = 1280
HALF = 640
RICOLS = 128
H = 128
EQ_PTS = 5632
PAD = 5632


def draw_counts(key, part):
    key = jax.random.fold_in(key, 11)
    jitter = jax.random.randint(key, (H,), 0, 3)
    pair_index = jnp.arange(H)
    jitter = jnp.where(pair_index == H - 1, 0, jitter)
    return (EQ_PTS - 4 * (H - 1 - pair_index) - 4 * jitter).astype(jnp.int32)


def draw_assign(key, part):
    key = jax.random.fold_in(key, 23)
    shuffled = jax.random.permutation(key, M // 2).astype(jnp.int32)
    paired = jnp.stack([shuffled, M - 1 - shuffled], axis=1).reshape(M)
    return paired.astype(jnp.int32)


def levels(key, dims, pieces, smallest, top_value):
    factor_of = 1.0
    for axis_at, shards_of in pieces:
        heights = jax.random.uniform(jax.random.fold_in(jax.random.fold_in(key, 6), axis_at), (shards_of,), jnp.float32, smallest / len(pieces), top_value / len(pieces))
        factor_of = factor_of * jnp.repeat(jnp.exp(heights), dims[axis_at] // shards_of).reshape((-1,) + (1,) * (len(dims) - 1 - axis_at))
    return factor_of


def noise(stream_key, dims, width, most, split=(), dtype=jnp.bfloat16):
    drawn = width * jax.random.normal(stream_key, dims, jnp.float32)
    if split:
        drawn = drawn * levels(stream_key, dims, split, -0.22, 0.18)
    return jnp.clip(drawn, -most, most).astype(dtype)


def setup_inputs(seed: int = 0) -> dict:
    streams_of = jax.random.split(jax.random.key(seed), 6)
    return {
        "spectra": noise(streams_of[0], (M, 2, RICOLS, HALF), (1.0 / M), 0.01171875, ((0, 128),), jnp.float32),
        "legendre": noise(streams_of[1], (H, M, 2, HALF), 1.0, 4.0, ((1, 128),), jnp.float32),
        "weights": jnp.clip(jnp.exp(jax.random.uniform(streams_of[2], (H,), jnp.float32, math.log(1.0), math.log(4.0))), 1.0, 4.0),
        "counts": draw_counts(jax.random.fold_in(streams_of[5], 71), 0),
        "assign": draw_assign(jax.random.fold_in(streams_of[5], 71), 0),
    }


HIGHEST_PRECISION = lax.Precision.HIGHEST


def block_size(padded):
    row_units = padded // 128
    chosen = 1
    for divisor in range(row_units, 0, -1):
        if row_units % divisor == 0 and divisor * 128 <= 1536:
            chosen = divisor
            break
    return chosen * 128


def degree_mask(numbers, wave_total, half_degrees):
    degree = 2 * lax.iota(jnp.int32, half_degrees)[None, None, :] + lax.iota(jnp.int32, 2)[None, :, None]
    return (degree < (wave_total - numbers)[:, None, None])[:, :, None, :]


def quadratic(physical_space_samples, atmosphere_layers):
    relative_rotation = physical_space_samples[:, :atmosphere_layers]
    velocity_spread = physical_space_samples[:, atmosphere_layers:2 * atmosphere_layers]
    thermal_state = physical_space_samples[:, 2 * atmosphere_layers:3 * atmosphere_layers]
    specific_humidity = physical_space_samples[:, 3 * atmosphere_layers:]
    return jnp.concatenate([relative_rotation * thermal_state, velocity_spread * thermal_state, thermal_state * specific_humidity, specific_humidity * velocity_spread], axis=1)


def latitude_cycle(fourier, point_count, numbers, padded, point_rows):
    wave_total = fourier.shape[0]
    columns = fourier.shape[1] // 2
    doubled = jnp.where(numbers == 0, 1.0, 2.0).astype(jnp.float32)[:, None]
    weighted = jnp.concatenate([fourier[:, :columns] * doubled, -fourier[:, columns:] * doubled], axis=0)
    step_angle = (2.0 * math.pi) / point_count.astype(jnp.float32)

    def add_block(summed, leading_row):
        points = leading_row + lax.iota(jnp.int32, point_rows)
        remainder_terms = (points[:, None] * numbers[None, :]) % point_count
        angles = remainder_terms.astype(jnp.float32) * step_angle
        basis_rows = jnp.concatenate([jnp.cos(angles), jnp.sin(angles)], axis=1)
        physical_space_samples = jnp.dot(basis_rows, weighted, precision=HIGHEST_PRECISION, preferred_element_type=jnp.float32)
        terms = jnp.where((points < point_count)[:, None], quadratic(physical_space_samples, columns // 4), 0.0)
        summed = summed + lax.dot_general(basis_rows, terms, (((0,), (0,)), ((), ())), precision=HIGHEST_PRECISION, preferred_element_type=jnp.float32)
        return summed, None

    starts = lax.iota(jnp.int32, padded // point_rows) * point_rows
    summed, unused = lax.scan(add_block, jnp.zeros((2 * wave_total, columns), jnp.float32), starts)
    inverse = 1.0 / point_count.astype(jnp.float32)
    return jnp.concatenate([summed[:wave_total] * inverse, -summed[wave_total:] * inverse], axis=1)


def reference(spectra, legendre, weights, counts, assign):
    wave_total = spectra.shape[0]
    valid_degrees = degree_mask(assign, wave_total, spectra.shape[3])
    masked = jnp.where(valid_degrees, spectra, 0.0)
    parity = jnp.einsum("jspq,sprq->jpsr", legendre, masked, precision=HIGHEST_PRECISION)
    fourier = jnp.stack([parity[:, 0] + parity[:, 1], parity[:, 0] - parity[:, 1]], axis=1)
    point_rows = block_size(PAD)

    def per_latitude(line_input):
        one_line, point_count = line_input
        return latitude_cycle(one_line, point_count, assign, PAD, point_rows)

    latitude_lines = fourier.reshape(-1, wave_total, fourier.shape[3])
    returned = lax.map(per_latitude, (latitude_lines, jnp.repeat(counts, 2))).reshape(fourier.shape)
    folded = weights[:, None, None, None] * jnp.stack([returned[:, 0] + returned[:, 1], returned[:, 0] - returned[:, 1]], axis=1)
    harmonic_products = jnp.einsum("jspq,jpsr->sprq", legendre, folded, precision=HIGHEST_PRECISION)
    return jnp.where(valid_degrees, harmonic_products, 0.0)
```

```python
import functools
import math

import jax
import jax.numpy as jnp
import ml_dtypes
import numpy as np
from jax import lax
from jax.experimental import pallas as pl
from jax.experimental.pallas import tpu as pltpu
from jax.sharding import PartitionSpec as P

WAVES = 1280
SPAN = 256
RADIX = 15
POINTS = RADIX * SPAN
PARTS = WAVES // SPAN
ROUNDS = RADIX // 2 + 1
SLOTS = 10
PAIRS = 128
HALF = 640
DEVICES = 128
OTHERS = DEVICES - 1
MESH = pl.DeviceIdType.MESH
F32 = jnp.float32
BF16 = jnp.bfloat16


def split_host(table):
    high = table.astype(ml_dtypes.bfloat16)
    low = (table - high.astype(np.float64)).astype(ml_dtypes.bfloat16)
    return high, low


@functools.cache
def tables():
    k1 = np.arange(ROUNDS)[:, None, None]
    k2 = np.arange(SPAN)[None, :, None]
    m2 = np.arange(SPAN)[None, None, :]
    angle = 2.0 * np.pi * ((m2 * (k1 + RADIX * k2)) % POINTS) / POINTS
    synthesis = np.concatenate([np.cos(angle), -np.sin(angle)], axis=2)
    analysis = np.ascontiguousarray(np.swapaxes(synthesis, 1, 2))
    turn = 2.0 * np.pi * ((np.arange(ROUNDS)[:, None] * np.arange(PARTS)[None, :]) % RADIX) / RADIX
    turns = np.concatenate([np.cos(turn), np.sin(turn)], axis=1).astype(np.float32).reshape(-1)
    return (*split_host(synthesis), *split_host(analysis), turns)


def halves(value):
    high = value.astype(BF16)
    low = (value - high.astype(F32)).astype(BF16)
    return high, low


def product(high, low, value, transposed=False):
    value_high, value_low = halves(value)
    if transposed:
        numbers = (((1,), (1,)), ((), ()))
        both = jnp.concatenate([value_high, value_low], axis=0)
        width = value.shape[0]
    else:
        numbers = (((1,), (0,)), ((), ()))
        both = jnp.concatenate([value_high, value_low], axis=1)
        width = value.shape[1]
    wide = lax.dot_general(high, both, numbers, preferred_element_type=F32)
    total = wide[:, :width] + wide[:, width:]
    if low is not None:
        total = total + lax.dot_general(low, value_high, numbers, preferred_element_type=F32)
    return total


def peer(step, lat, wave):
    mixed = lax.rem(step * 37, DEVICES)
    z = lax.rem(lat // 8 + mixed // 32, 4)
    y = lax.rem(lax.rem(lat // 2, 4) + lax.rem(mixed // 8, 4), 4)
    core = lax.rem(lax.rem(lat, 2) + lax.rem(mixed // 4, 2), 2)
    x = lax.rem(wave + lax.rem(mixed, 4), 4)
    return z * 8 + y * 2 + core, x


def valid_degrees(number, parity, rows):
    degree = 2 * lax.broadcasted_iota(jnp.int32, (rows, HALF), 1) + parity
    return degree < WAVES - number


def grid_kernel(
    legendre, spectra, assign_scalar, assign_rows, synthesis_high, synthesis_low, analysis_high, analysis_low, turns,
    returned,
    functions, coefficients, forward_high, forward_low, backward_high, backward_low, order, order_back,
    outgoing, incoming, results, waves, sums, load_sem, table_sem, send_sem, receive_sem, own_sem,
):
    lat, wave = lax.axis_index("lat"), lax.axis_index("wave")
    me = lat * 4 + wave
    barrier = pltpu.get_barrier_semaphore()

    def function_copy(slot, parity):
        return pltpu.make_async_copy(legendre.at[:, slot, parity], functions.at[slot, parity], load_sem.at[slot, parity])

    def coefficient_copy(slot, half):
        return pltpu.make_async_copy(
            spectra.at[slot, :, :, :, half], coefficients.at[slot, :, :, half], load_sem.at[slot, 2 + half]
        )

    def start_loads(slot, carry):
        for place in range(2):
            coefficient_copy(slot, place).start()
            function_copy(slot, place).start()
        return carry

    lax.fori_loop(0, SLOTS, start_loads, 0)
    table_copies = [
        pltpu.make_async_copy(source, target, table_sem.at[place])
        for place, (source, target) in enumerate(
            (
                (synthesis_high, forward_high),
                (synthesis_low, forward_low),
                (analysis_high, backward_high),
                (analysis_low, backward_low),
            )
        )
    ]
    for copy in table_copies:
        copy.start()

    def greet(step, carry):
        other_lat, other_wave = peer(step, lat, wave)
        pl.semaphore_signal(barrier, inc=1, device_id=(other_lat, other_wave), device_id_type=MESH)
        return carry

    lax.fori_loop(1, DEVICES, greet, 0)

    lane = lax.broadcasted_iota(jnp.int32, (PAIRS, 128), 1)
    even_block = lax.rem(lane // 32, 2) == 0

    def to_fourier(slot, carry):
        for place in range(2):
            coefficient_copy(slot, place).wait()
            function_copy(slot, place).wait()
        number = assign_scalar[me * SLOTS + slot]
        parts = []
        for parity in range(2):
            values = coefficients[slot, parity].reshape(128, HALF)
            masked = jnp.where(valid_degrees(number, parity, 128), values, 0.0)
            high, low = halves(functions[slot, parity])
            parts.append(product(high, low, masked, transposed=True))
        north, south = parts[0] + parts[1], parts[0] - parts[1]
        rows = pl.ds(slot, PAIRS, stride=SLOTS)
        outgoing[0, rows, :] = jnp.where(even_block, north, pltpu.roll(south, 32, 1))
        outgoing[1, rows, :] = jnp.where(even_block, pltpu.roll(north, 96, 1), south)
        return carry

    lax.fori_loop(0, SLOTS, to_fourier, 0)
    pl.semaphore_wait(barrier, OTHERS)

    def send(source, target, place):
        def one(step, carry):
            other_lat, other_wave = peer(step, lat, wave)
            other = other_lat * 4 + other_wave
            pltpu.make_async_remote_copy(
                source.at[pl.ds(other * SLOTS, SLOTS)],
                target.at[pl.ds(me * SLOTS, SLOTS)],
                send_sem.at[place],
                receive_sem.at[place],
                device_id=(other_lat, other_wave),
                device_id_type=MESH,
            ).start()
            return carry

        lax.fori_loop(1, DEVICES, one, 0)
        mine = pl.ds(me * SLOTS, SLOTS)
        pltpu.make_async_copy(source.at[mine], target.at[mine], own_sem.at[place]).start()

    def settle(source, target, place, sem):
        rows = pl.ds(0, OTHERS * SLOTS)
        pltpu.make_async_copy(source.at[rows], target.at[rows], sem.at[place]).wait()

    def own(source, target, place):
        mine = pl.ds(me * SLOTS, SLOTS)
        pltpu.make_async_copy(source.at[mine], target.at[mine], own_sem.at[place]).wait()

    for half in range(2):
        send(outgoing.at[half], incoming.at[half], half)

    column_of = jnp.transpose(assign_rows[...].astype(F32))

    def build_order(block, carry):
        rows = pl.ds(pl.multiple_of(block * 128, 128), 128)
        number = block * 128 + lax.broadcasted_iota(jnp.int32, (128, 128), 0)
        for place in range(WAVES // 128):
            held = assign_rows[pl.ds(place, 1), :]
            order[rows, pl.ds(place * 128, 128)] = jnp.where(number == held, 1.0, 0.0).astype(BF16)
        return carry

    lax.fori_loop(0, WAVES // 128, build_order, 0)
    for block in range(WAVES // 128):
        held = jnp.broadcast_to(column_of[:, block : block + 1], (128, 128))
        for place in range(WAVES // 128):
            number = (place * 128 + lax.broadcasted_iota(jnp.int32, (128, 128), 1)).astype(F32)
            order_back[pl.ds(block * 128, 128), pl.ds(place * 128, 128)] = jnp.where(held == number, 1.0, 0.0).astype(BF16)

    for copy in table_copies:
        copy.wait()

    span_lane = lax.broadcasted_iota(jnp.int32, (SPAN, 128), 1)
    left = span_lane < 64
    sign = jnp.where(left, 1.0, -1.0)
    field = lax.rem(span_lane // 8, 4)
    first_row = lax.broadcasted_iota(jnp.int32, (SPAN, 128), 0) == 0

    def cross(value):
        return pltpu.roll(value, 64, 1) + sign * value

    for half in range(2):
        settle(outgoing.at[half], incoming.at[half], half, receive_sem)
        own(outgoing.at[half], incoming.at[half], half)
        received = incoming[half]
        received_both = jnp.concatenate(halves(received), axis=1)

        def to_order(part, carry):
            rows = pl.ds(pl.multiple_of(part * SPAN, SPAN), SPAN)
            wide = jnp.dot(order[rows, :], received_both, preferred_element_type=F32)
            value = wide[:, :128] + wide[:, 128:]
            waves[part] = jnp.where(jnp.logical_and(first_row, part == 0), 0.5 * value, value)
            return carry

        lax.fori_loop(0, PARTS, to_order, 0)
        sums[...] = jnp.zeros_like(sums)

        def turn_round(k1, carry):
            cosines = [turns[k1 * 2 * PARTS + part] for part in range(PARTS)]
            sines = [turns[k1 * 2 * PARTS + PARTS + part] for part in range(PARTS)]
            c_sum = waves[0]
            s_sum = sines[1] * waves[1]
            for part in range(1, PARTS):
                c_sum = c_sum + cosines[part] * waves[part]
                if part > 1:
                    s_sum = s_sum + sines[part] * waves[part]
            operand = jnp.concatenate([jnp.where(left, c_sum, -s_sum), jnp.where(left, s_sum, c_sum)], axis=0)
            points = cross(product(forward_high[k1], forward_low[k1], operand))
            other = jnp.where(
                field == 0,
                pltpu.roll(points, 112, 1),
                jnp.where(field == 3, pltpu.roll(points, 16, 1), pltpu.roll(points, 120, 1)),
            )
            doubled = jnp.logical_and(k1 == 0, jnp.logical_not(left))
            terms = cross(jnp.where(doubled, 0.0, points * other))
            found = product(backward_high[k1], backward_low[k1], terms)
            even, odd = found[:SPAN], found[SPAN:]
            c_part = jnp.where(left, even, odd)
            s_part = jnp.where(left, odd, -even)
            sums[0] += c_part
            for part in range(1, PARTS):
                sums[part] += cosines[part] * c_part + sines[part] * s_part
            return carry

        lax.fori_loop(0, ROUNDS, turn_round, 0)
        found_both = jnp.concatenate(halves(sums[...].reshape(WAVES, 128)), axis=1)

        def to_slots(part, carry):
            rows = pl.ds(pl.multiple_of(part * SPAN, SPAN), SPAN)
            wide = jnp.dot(order_back[rows, :], found_both, preferred_element_type=F32)
            results[half, rows, :] = wide[:, :128] + wide[:, 128:]
            return carry

        lax.fori_loop(0, PARTS, to_slots, 0)
        send(results.at[half], returned.at[half], 2 + half)

    for half in range(2):
        settle(outgoing.at[half], incoming.at[half], half, send_sem)
    for half in range(2):
        settle(results.at[half], returned.at[half], 2 + half, receive_sem)
        own(results.at[half], returned.at[half], 2 + half)
        settle(results.at[half], returned.at[half], 2 + half, send_sem)


def harmonic_kernel(own_numbers, legendre, returned, weights, out, functions, load_sem):
    slot = pl.program_id(0)

    def function_copy(place, parity):
        return pltpu.make_async_copy(legendre.at[:, place, parity], functions.at[place, parity], load_sem.at[place, parity])

    @pl.when(slot == 0)
    def _():
        for place in range(SLOTS):
            for parity in range(2):
                function_copy(place, parity).start()

    rows = pl.ds(slot, PAIRS, stride=SLOTS)
    first, second = returned[0, rows, :], returned[1, rows, :]
    even_block = lax.rem(lax.broadcasted_iota(jnp.int32, (PAIRS, 128), 1) // 32, 2) == 0
    first_other, second_other = pltpu.roll(first, 96, 1), pltpu.roll(second, 32, 1)
    scale = weights[...] * (4.0 / POINTS)
    for parity in range(2):
        if parity == 0:
            folded = jnp.where(even_block, first + first_other, second_other + second)
        else:
            folded = jnp.where(even_block, first - first_other, second_other - second)
        high, low = halves(jnp.transpose(folded) * scale)
        function_copy(slot, parity).wait()
        function_high, function_low = halves(functions[slot, parity])
        total = jnp.dot(
            jnp.concatenate([high, low], axis=1),
            jnp.concatenate([function_high, function_high], axis=0),
            preferred_element_type=F32,
        ) + jnp.dot(high, function_low, preferred_element_type=F32)
        total = jnp.where(valid_degrees(own_numbers[slot], parity, 128), total, 0.0)
        for part in range(2):
            for half in range(2):
                for field in range(4):
                    source = ((part * 2 + half) * 4 + field) * 8
                    target = ((part * 4 + field) * 2 + half) * 8
                    out[0, parity, target : target + 8, :] = total[source : source + 8]


def body(spectra, legendre, weights, counts, assign):
    del counts
    *tables_of, turns = tables()
    any_space = pl.BlockSpec(memory_space=pl.ANY)
    scalar = pl.BlockSpec(memory_space=pltpu.SMEM)
    vector = pl.BlockSpec(memory_space=pltpu.VMEM)
    place = lax.axis_index(("lat", "wave"))
    own_numbers = lax.dynamic_slice_in_dim(assign, place * SLOTS, SLOTS)
    returned = pl.pallas_call(
        grid_kernel,
        out_shape=jax.ShapeDtypeStruct((2, WAVES, 128), F32),
        in_specs=[any_space, any_space, scalar, vector, any_space, any_space, any_space, any_space, scalar],
        out_specs=any_space,
        scratch_shapes=[
            pltpu.VMEM((SLOTS, 2, PAIRS, HALF), F32),
            pltpu.VMEM((SLOTS, 2, 2, 2, 4, 8, HALF), F32),
            pltpu.VMEM((ROUNDS, SPAN, 2 * SPAN), BF16),
            pltpu.VMEM((ROUNDS, SPAN, 2 * SPAN), BF16),
            pltpu.VMEM((ROUNDS, 2 * SPAN, SPAN), BF16),
            pltpu.VMEM((ROUNDS, 2 * SPAN, SPAN), BF16),
            pltpu.VMEM((WAVES, WAVES), BF16),
            pltpu.VMEM((WAVES, WAVES), BF16),
            pltpu.VMEM((2, WAVES, 128), F32),
            pltpu.VMEM((2, WAVES, 128), F32),
            pltpu.VMEM((2, WAVES, 128), F32),
            pltpu.VMEM((PARTS, SPAN, 128), F32),
            pltpu.VMEM((PARTS, SPAN, 128), F32),
            pltpu.SemaphoreType.DMA((SLOTS, 4)),
            pltpu.SemaphoreType.DMA((4,)),
            pltpu.SemaphoreType.DMA((4,)),
            pltpu.SemaphoreType.DMA((4,)),
            pltpu.SemaphoreType.DMA((4,)),
        ],
        compiler_params=pltpu.CompilerParams(collective_id=0, has_side_effects=True, vmem_limit_bytes=56 << 20),
        name="grid_round_trip",
    )(
        legendre,
        spectra.reshape(SLOTS, 2, 2, 4, 2, 8, HALF),
        assign,
        jnp.pad(assign.reshape(WAVES // 128, 128), ((0, 6), (0, 0))),
        *(jnp.asarray(table) for table in tables_of),
        jnp.asarray(turns),
    )
    return pl.pallas_call(
        harmonic_kernel,
        grid=(SLOTS,),
        out_shape=jax.ShapeDtypeStruct((SLOTS, 2, 128, HALF), F32),
        in_specs=[
            scalar,
            any_space,
            pl.BlockSpec((2, WAVES, 128), lambda slot: (0, 0, 0)),
            pl.BlockSpec((1, PAIRS), lambda slot: (0, 0)),
        ],
        out_specs=pl.BlockSpec((1, 2, 128, HALF), lambda slot: (slot, 0, 0, 0)),
        scratch_shapes=[pltpu.VMEM((SLOTS, 2, PAIRS, HALF), F32), pltpu.SemaphoreType.DMA((SLOTS, 2))],
        compiler_params=pltpu.CompilerParams(vmem_limit_bytes=40 << 20),
        name="harmonics",
    )(own_numbers, legendre, returned, weights.reshape(1, PAIRS))


def solution(mesh):
    placed = (
        P(("lat", "wave"), None, None, None),
        P(None, ("lat", "wave"), None, None),
        P(),
        P("lat"),
        P(),
    )
    return jax.shard_map(
        body,
        mesh=mesh,
        in_specs=placed,
        out_specs=P(("lat", "wave"), None, None, None),
        check_vma=False,
    )
```

```python
import functools
import math

import jax
import jax.numpy as jnp
import ml_dtypes
import numpy as np
from jax import lax
from jax.experimental import pallas as pl
from jax.experimental.pallas import tpu as pltpu
from jax.sharding import PartitionSpec as P

WAVES = 1280
SPAN = 256
RADIX = 15
POINTS = RADIX * SPAN
PARTS = WAVES // SPAN
ROUNDS = RADIX // 2 + 1
SLOTS = 10
PAIRS = 128
HALF = 640
DEVICES = 128
OTHERS = DEVICES - 1
MESH = pl.DeviceIdType.MESH
F32 = jnp.float32
BF16 = jnp.bfloat16


def stacked(table):
    high = table.astype(ml_dtypes.bfloat16)
    low = (table - high.astype(np.float64)).astype(ml_dtypes.bfloat16)
    return np.concatenate([high, low], axis=1)


def turn(k1, part):
    angle = 2.0 * math.pi * ((k1 * part) % RADIX) / RADIX
    return math.cos(angle), math.sin(angle)


@functools.cache
def tables():
    k1 = np.arange(ROUNDS)[:, None, None]
    k2 = np.arange(SPAN)[None, :, None]
    m2 = np.arange(SPAN)[None, None, :]
    angle = 2.0 * np.pi * ((m2 * (k1 + RADIX * k2)) % POINTS) / POINTS
    synthesis = np.concatenate([np.cos(angle), -np.sin(angle)], axis=2)
    analysis = np.ascontiguousarray(np.swapaxes(synthesis, 1, 2))
    return stacked(synthesis), stacked(analysis)


def halves(value):
    high = value.astype(BF16)
    low = (value - high.astype(F32)).astype(BF16)
    return high, low


def row_product(high, low, value):
    value_high, value_low = halves(value)
    numbers = (((1,), (1,)), ((), ()))
    both = jnp.concatenate([value_high, value_low], axis=0)
    width = value.shape[0]
    wide = lax.dot_general(high, both, numbers, preferred_element_type=F32)
    total = wide[:, :width] + wide[:, width:]
    return total + lax.dot_general(low, value_high, numbers, preferred_element_type=F32)


def table_product(table, value):
    wide = jnp.dot(table, jnp.concatenate(halves(value), axis=1), preferred_element_type=F32)
    rows, width = wide.shape[0] // 2, value.shape[1]
    return wide[:rows, :width] + (wide[:rows, width:] + wide[rows:, :width])


def peer(step, lat, wave):
    mixed = lax.rem(step * 37, DEVICES)
    z = lax.rem(lat // 8 + mixed // 32, 4)
    y = lax.rem(lax.rem(lat // 2, 4) + lax.rem(mixed // 8, 4), 4)
    core = lax.rem(lax.rem(lat, 2) + lax.rem(mixed // 4, 2), 2)
    x = lax.rem(wave + lax.rem(mixed, 4), 4)
    return z * 8 + y * 2 + core, x


def valid_degrees(number, parity, rows):
    degree = 2 * lax.broadcasted_iota(jnp.int32, (rows, HALF), 1) + parity
    return degree < WAVES - number


def grid_kernel(
    legendre, spectra, assign_scalar, assign, synthesis_table, analysis_table,
    returned, function_high, function_low,
    functions, coefficients, synthesis, analysis, assign_rows, order,
    outgoing, incoming, results, waves, sums, load_sem, table_sem, send_sem, receive_sem, own_sem,
):
    lat, wave = lax.axis_index("lat"), lax.axis_index("wave")
    me = lat * 4 + wave
    barrier = pltpu.get_barrier_semaphore()

    def function_copy(slot, parity):
        return pltpu.make_async_copy(legendre.at[:, slot, parity], functions.at[slot, parity], load_sem.at[slot, parity])

    def coefficient_copy(slot, half):
        return pltpu.make_async_copy(
            spectra.at[slot, :, :, :, half], coefficients.at[slot, :, :, half], load_sem.at[slot, 2 + half]
        )

    def start_loads(slot, carry):
        for place in range(2):
            coefficient_copy(slot, place).start()
            function_copy(slot, place).start()
        return carry

    lax.fori_loop(0, SLOTS, start_loads, 0)
    row_copies = [
        pltpu.make_async_copy(assign.at[pl.ds(row * 128, 128)], assign_rows.at[row], table_sem.at[2 + row])
        for row in range(WAVES // 128)
    ]
    for copy in row_copies:
        copy.start()

    def greet(step, carry):
        other_lat, other_wave = peer(step, lat, wave)
        pl.semaphore_signal(barrier, inc=1, device_id=(other_lat, other_wave), device_id_type=MESH)
        return carry

    lax.fori_loop(1, DEVICES, greet, 0)

    lane = lax.broadcasted_iota(jnp.int32, (PAIRS, 128), 1)
    even_block = lax.rem(lane // 32, 2) == 0

    def to_fourier(slot, carry):
        for place in range(2):
            coefficient_copy(slot, place).wait()
            function_copy(slot, place).wait()
        number = assign_scalar[me * SLOTS + slot]
        parts = []
        for parity in range(2):
            values = coefficients[slot, parity].reshape(128, HALF)
            masked = jnp.where(valid_degrees(number, parity, 128), values, 0.0)
            high, low = halves(functions[slot, parity])
            function_high[slot, parity] = high
            function_low[slot, parity] = low
            parts.append(row_product(high, low, masked))
        north, south = parts[0] + parts[1], parts[0] - parts[1]
        rows = pl.ds(slot, PAIRS, stride=SLOTS)
        outgoing[0, rows, :] = jnp.where(even_block, north, pltpu.roll(south, 32, 1))
        outgoing[1, rows, :] = jnp.where(even_block, pltpu.roll(north, 96, 1), south)
        return carry

    lax.fori_loop(0, SLOTS, to_fourier, 0)
    pl.semaphore_wait(barrier, OTHERS)

    def send(source, target, place, prepare=None):
        def one(step, carry):
            other_lat, other_wave = peer(step, lat, wave)
            other = other_lat * 4 + other_wave
            if prepare is not None:
                prepare(other)
            pltpu.make_async_remote_copy(
                source.at[pl.ds(other * SLOTS, SLOTS)],
                target.at[pl.ds(me * SLOTS, SLOTS)],
                send_sem.at[place],
                receive_sem.at[place],
                device_id=(other_lat, other_wave),
                device_id_type=MESH,
            ).start()
            return carry

        lax.fori_loop(1, DEVICES, one, 0)
        if prepare is not None:
            prepare(me)
        mine = pl.ds(me * SLOTS, SLOTS)
        pltpu.make_async_copy(source.at[mine], target.at[mine], own_sem.at[place]).start()

    def settle(source, target, place, sem):
        rows = pl.ds(0, OTHERS * SLOTS)
        pltpu.make_async_copy(source.at[rows], target.at[rows], sem.at[place]).wait()

    def own(source, target, place):
        mine = pl.ds(me * SLOTS, SLOTS)
        pltpu.make_async_copy(source.at[mine], target.at[mine], own_sem.at[place]).wait()

    for half in range(2):
        send(outgoing.at[half], incoming.at[half], half)

    table_copies = [
        pltpu.make_async_copy(synthesis_table, synthesis, table_sem.at[0]),
        pltpu.make_async_copy(analysis_table, analysis, table_sem.at[1]),
    ]
    for copy in table_copies:
        copy.start()
    for copy in row_copies:
        copy.wait()

    def build_order(block, carry):
        rows = pl.ds(pl.multiple_of(block * 128, 128), 128)
        number = block * 128 + lax.broadcasted_iota(jnp.int32, (128, 128), 0)
        for place in range(WAVES // 128):
            held = assign_rows[pl.ds(place, 1), :]
            order[rows, pl.ds(place * 128, 128)] = jnp.where(number == held, 1.0, 0.0).astype(BF16)
        return carry

    lax.fori_loop(0, WAVES // 128, build_order, 0)
    for copy in table_copies:
        copy.wait()

    span_lane = lax.broadcasted_iota(jnp.int32, (SPAN, 128), 1)
    left = span_lane < 64
    sign = jnp.where(left, 1.0, -1.0)
    field = lax.rem(span_lane // 8, 4)
    first_row = lax.broadcasted_iota(jnp.int32, (SPAN, 128), 0) == 0

    def cross(value):
        return pltpu.roll(value, 64, 1) + sign * value

    for half in range(2):
        settle(outgoing.at[half], incoming.at[half], half, receive_sem)
        own(outgoing.at[half], incoming.at[half], half)
        received = incoming[half]
        received_both = jnp.concatenate(halves(received), axis=1)

        for part in range(PARTS):
            wide = jnp.dot(order[pl.ds(part * SPAN, SPAN), :], received_both, preferred_element_type=F32)
            value = wide[:, :128] + wide[:, 128:]
            waves[part] = jnp.where(first_row, 0.5 * value, value) if part == 0 else value

        for k1 in range(ROUNDS):
            c_sum, s_sum = waves[0], 0.0 * waves[0] if k1 == 0 else 0.0
            for part in range(1, PARTS):
                cosine, sine = turn(k1, part)
                c_sum = c_sum + cosine * waves[part]
                if k1 > 0:
                    s_sum = s_sum + sine * waves[part]
            operand = jnp.concatenate([jnp.where(left, c_sum, -s_sum), jnp.where(left, s_sum, c_sum)], axis=0)
            points = cross(table_product(synthesis[k1], operand))
            other = jnp.where(
                field == 0,
                pltpu.roll(points, 112, 1),
                jnp.where(field == 3, pltpu.roll(points, 16, 1), pltpu.roll(points, 120, 1)),
            )
            terms = points * other
            if k1 == 0:
                terms = jnp.where(left, terms, 0.0)
            found = table_product(analysis[k1], cross(terms))
            even, odd = found[:SPAN], found[SPAN:]
            c_part = jnp.where(left, even, odd)
            s_part = jnp.where(left, odd, -even)
            if k1 == 0:
                for part in range(PARTS):
                    sums[pl.ds(part * SPAN, SPAN), :] = c_part
            else:
                sums[pl.ds(0, SPAN), :] += c_part
                for part in range(1, PARTS):
                    cosine, sine = turn(k1, part)
                    sums[pl.ds(part * SPAN, SPAN), :] += cosine * c_part + sine * s_part

        def to_slots(other):
            for slot in range(SLOTS):
                row = other * SLOTS + slot
                results[half, pl.ds(row, 1), :] = sums[pl.ds(assign_scalar[row], 1), :]

        send(results.at[half], returned.at[half], 2 + half, to_slots)

    for half in range(2):
        settle(outgoing.at[half], incoming.at[half], half, send_sem)
    for half in range(2):
        settle(results.at[half], returned.at[half], 2 + half, receive_sem)
        own(results.at[half], returned.at[half], 2 + half)
        settle(results.at[half], returned.at[half], 2 + half, send_sem)


def harmonic_kernel(assign, function_high, function_low, returned, weights, out, harmonics, store_sem):
    first_number = (lax.axis_index("lat") * 4 + lax.axis_index("wave")) * SLOTS
    even_block = lax.rem(lax.broadcasted_iota(jnp.int32, (PAIRS, 128), 1) // 32, 2) == 0
    scale = weights[...] * (4.0 / POINTS)

    def store_copy(slot):
        return pltpu.make_async_copy(harmonics.at[slot], out.at[slot], store_sem.at[slot])

    def to_harmonics(slot, carry):
        rows = pl.ds(slot, PAIRS, stride=SLOTS)
        first, second = returned[0, rows, :], returned[1, rows, :]
        first_other, second_other = pltpu.roll(first, 96, 1), pltpu.roll(second, 32, 1)
        for parity in range(2):
            if parity == 0:
                folded = jnp.where(even_block, first + first_other, second_other + second)
            else:
                folded = jnp.where(even_block, first - first_other, second_other - second)
            high, low = halves(jnp.transpose(folded) * scale)
            functions = function_high[slot, parity]
            total = jnp.dot(
                jnp.concatenate([high, low], axis=1),
                jnp.concatenate([functions, functions], axis=0),
                preferred_element_type=F32,
            ) + jnp.dot(high, function_low[slot, parity], preferred_element_type=F32)
            total = jnp.where(valid_degrees(assign[first_number + slot], parity, 128), total, 0.0)
            for part in range(2):
                for half in range(2):
                    for field in range(4):
                        source = ((part * 2 + half) * 4 + field) * 8
                        target = ((part * 4 + field) * 2 + half) * 8
                        harmonics[slot, parity, target : target + 8, :] = total[source : source + 8]
        store_copy(slot).start()
        return carry

    lax.fori_loop(0, SLOTS, to_harmonics, 0)
    for slot in range(SLOTS):
        store_copy(slot).wait()


def body(spectra, legendre, weights, counts, assign):
    del counts
    synthesis, analysis = tables()
    any_space = pl.BlockSpec(memory_space=pl.ANY)
    scalar = pl.BlockSpec(memory_space=pltpu.SMEM)
    vector = pl.BlockSpec(memory_space=pltpu.VMEM)
    returned, function_high, function_low = pl.pallas_call(
        grid_kernel,
        out_shape=[
            jax.ShapeDtypeStruct((2, WAVES, 128), F32),
            jax.ShapeDtypeStruct((SLOTS, 2, PAIRS, HALF), BF16),
            jax.ShapeDtypeStruct((SLOTS, 2, PAIRS, HALF), BF16),
        ],
        in_specs=[any_space, any_space, scalar, any_space, any_space, any_space],
        out_specs=[vector, vector, vector],
        scratch_shapes=[
            pltpu.VMEM((SLOTS, 2, PAIRS, HALF), F32),
            pltpu.VMEM((SLOTS, 2, 2, 2, 4, 8, HALF), F32),
            pltpu.VMEM((ROUNDS, 2 * SPAN, 2 * SPAN), BF16),
            pltpu.VMEM((ROUNDS, 4 * SPAN, SPAN), BF16),
            pltpu.VMEM((16, 128), jnp.int32),
            pltpu.VMEM((WAVES, WAVES), BF16),
            pltpu.VMEM((2, WAVES, 128), F32),
            pltpu.VMEM((2, WAVES, 128), F32),
            pltpu.VMEM((2, WAVES, 128), F32),
            pltpu.VMEM((PARTS, SPAN, 128), F32),
            pltpu.VMEM((WAVES, 128), F32),
            pltpu.SemaphoreType.DMA((SLOTS, 4)),
            pltpu.SemaphoreType.DMA((2 + WAVES // 128,)),
            pltpu.SemaphoreType.DMA((4,)),
            pltpu.SemaphoreType.DMA((4,)),
            pltpu.SemaphoreType.DMA((4,)),
        ],
        compiler_params=pltpu.CompilerParams(collective_id=0, has_side_effects=True, vmem_limit_bytes=44 << 20),
        name="grid_round_trip",
    )(legendre, spectra.reshape(SLOTS, 2, 2, 4, 2, 8, HALF), assign, assign, jnp.asarray(synthesis), jnp.asarray(analysis))
    return pl.pallas_call(
        harmonic_kernel,
        out_shape=jax.ShapeDtypeStruct((SLOTS, 2, 128, HALF), F32),
        in_specs=[scalar, vector, vector, vector, vector],
        out_specs=any_space,
        scratch_shapes=[pltpu.VMEM((SLOTS, 2, 128, HALF), F32), pltpu.SemaphoreType.DMA((SLOTS,))],
        compiler_params=pltpu.CompilerParams(vmem_limit_bytes=32 << 20),
        name="harmonics",
    )(assign, function_high, function_low, returned, weights.reshape(1, PAIRS))


def solution(mesh):
    placed = (
        P(("lat", "wave"), None, None, None),
        P(None, ("lat", "wave"), None, None),
        P(),
        P("lat"),
        P(),
    )
    return jax.shard_map(
        body,
        mesh=mesh,
        in_specs=placed,
        out_specs=P(("lat", "wave"), None, None, None),
        check_vma=False,
    )
```

```python
import functools
import math

import jax
import jax.numpy as jnp
import ml_dtypes
import numpy as np
from jax import lax
from jax.experimental import pallas as pl
from jax.experimental.pallas import tpu as pltpu
from jax.sharding import PartitionSpec as P

WAVES = 1280
SPAN = 256
RADIX = 15
POINTS = RADIX * SPAN
PARTS = WAVES // SPAN
ROUNDS = RADIX // 2 + 1
SLOTS = 10
EARLY = 5
PAIRS = 128
HALF = 640
DEVICES = 128
OTHERS = DEVICES - 1
MESH = pl.DeviceIdType.MESH
F32 = jnp.float32
BF16 = jnp.bfloat16


def stacked(table):
    high = table.astype(ml_dtypes.bfloat16)
    low = (table - high.astype(np.float64)).astype(ml_dtypes.bfloat16)
    return np.concatenate([high, low], axis=1)


def turn(k1, part):
    angle = 2.0 * math.pi * ((k1 * part) % RADIX) / RADIX
    return math.cos(angle), math.sin(angle)


@functools.cache
def tables():
    k1 = np.arange(ROUNDS)[:, None, None]
    k2 = np.arange(SPAN)[None, :, None]
    m2 = np.arange(SPAN)[None, None, :]
    angle = 2.0 * np.pi * ((m2 * (k1 + RADIX * k2)) % POINTS) / POINTS
    synthesis = np.concatenate([np.cos(angle), -np.sin(angle)], axis=2)
    analysis = np.ascontiguousarray(np.swapaxes(synthesis, 1, 2))
    return stacked(synthesis), stacked(analysis)


def halves(value):
    high = value.astype(BF16)
    low = (value - high.astype(F32)).astype(BF16)
    return high, low


def row_product(high, low, value):
    value_high, value_low = halves(value)
    numbers = (((1,), (1,)), ((), ()))
    both = jnp.concatenate([value_high, value_low], axis=0)
    width = value.shape[0]
    wide = lax.dot_general(high, both, numbers, preferred_element_type=F32)
    total = wide[:, :width] + wide[:, width:]
    return total + lax.dot_general(low, value_high, numbers, preferred_element_type=F32)


def table_product(table, value):
    wide = jnp.dot(table, jnp.concatenate(halves(value), axis=1), preferred_element_type=F32)
    rows, width = wide.shape[0] // 2, value.shape[1]
    return wide[:rows, :width] + (wide[:rows, width:] + wide[rows:, :width])


def for_others(lat, wave, act):
    z, y, core = lat // 8, lax.rem(lat // 2, 4), lax.rem(lat, 2)
    cores = [core, 1 - core]
    xs = [lax.rem(wave + offset, 4) for offset in range(4)]

    def group(step, carry, places=range(8)):
        z_step, y_step = z + step // 4, y + lax.rem(step, 4)
        for place in places:
            other_z, other_y = lax.rem(z_step + place, 4), lax.rem(y_step + place // 2, 4)
            act(other_z * 8 + other_y * 2 + cores[place // 4], xs[place % 4])
        return carry

    group(0, 0, range(1, 8))
    lax.fori_loop(1, 16, group, 0)


def valid_degrees(number, parity, rows):
    degree = 2 * lax.broadcasted_iota(jnp.int32, (rows, HALF), 1) + parity
    return degree < WAVES - number


def grid_kernel(
    legendre, spectra, assign, synthesis_table, analysis_table,
    returned, function_high, function_low,
    functions, coefficients, synthesis, analysis, assign_scalar, assign_rows, order,
    outgoing, incoming, results, waves, sums, load_sem, table_sem, send_sem, receive_sem, own_sem,
):
    lat, wave = lax.axis_index("lat"), lax.axis_index("wave")
    me = lat * 4 + wave
    barrier = pltpu.get_barrier_semaphore()

    def function_copy(slot, parity):
        return pltpu.make_async_copy(legendre.at[:, slot, parity], functions.at[slot, parity], load_sem.at[slot, parity])

    def coefficient_copy(slot, half):
        return pltpu.make_async_copy(
            spectra.at[slot, :, :, :, half], coefficients.at[slot, :, :, half], load_sem.at[slot, 2 + half]
        )

    scalar_copy = pltpu.make_async_copy(assign, assign_scalar, table_sem.at[2 + WAVES // 128])
    scalar_copy.start()

    def start_loads(slot, carry):
        for place in range(2):
            coefficient_copy(slot, place).start()
            function_copy(slot, place).start()
        return carry

    lax.fori_loop(0, SLOTS, start_loads, 0)
    row_copies = [
        pltpu.make_async_copy(assign.at[pl.ds(row * 128, 128)], assign_rows.at[row], table_sem.at[2 + row])
        for row in range(WAVES // 128)
    ]
    for copy in row_copies:
        copy.start()

    def greet(other_lat, other_wave):
        pl.semaphore_signal(barrier, inc=1, device_id=(other_lat, other_wave), device_id_type=MESH)

    for_others(lat, wave, greet)

    lane = lax.broadcasted_iota(jnp.int32, (PAIRS, 128), 1)
    even_block = lax.rem(lane // 32, 2) == 0

    def to_fourier(slot, carry):
        for place in range(2):
            coefficient_copy(slot, place).wait()
            function_copy(slot, place).wait()
        number = assign_scalar[me * SLOTS + slot]
        parts = []
        for parity in range(2):
            values = coefficients[slot, parity].reshape(128, HALF)
            masked = jnp.where(valid_degrees(number, parity, 128), values, 0.0)
            high, low = halves(functions[slot, parity])
            function_high[slot, parity] = high
            function_low[slot, parity] = low
            parts.append(row_product(high, low, masked))
        north, south = parts[0] + parts[1], parts[0] - parts[1]
        rows = pl.ds(slot, PAIRS, stride=SLOTS)
        outgoing[0, rows, :] = jnp.where(even_block, north, pltpu.roll(south, 32, 1))
        outgoing[1, rows, :] = jnp.where(even_block, pltpu.roll(north, 96, 1), south)
        return carry

    def send(source, target, place, first=0, count=SLOTS, prepare=None):
        def one(other_lat, other_wave):
            other = other_lat * 4 + other_wave
            if prepare is not None:
                prepare(other)
            pltpu.make_async_remote_copy(
                source.at[pl.ds(other * SLOTS + first, count)],
                target.at[pl.ds(me * SLOTS + first, count)],
                send_sem.at[place],
                receive_sem.at[place],
                device_id=(other_lat, other_wave),
                device_id_type=MESH,
            ).start()

        for_others(lat, wave, one)
        if prepare is not None:
            prepare(me)
        mine = pl.ds(me * SLOTS + first, count)
        pltpu.make_async_copy(source.at[mine], target.at[mine], own_sem.at[place]).start()

    def settle(source, target, place, sem, count=SLOTS):
        rows = pl.ds(0, OTHERS * count)
        pltpu.make_async_copy(source.at[rows], target.at[rows], sem.at[place]).wait()

    def own(source, target, place, first=0, count=SLOTS):
        mine = pl.ds(me * SLOTS + first, count)
        pltpu.make_async_copy(source.at[mine], target.at[mine], own_sem.at[place]).wait()

    scalar_copy.wait()
    lax.fori_loop(0, EARLY, to_fourier, 0)
    pl.semaphore_wait(barrier, OTHERS)
    send(outgoing.at[0], incoming.at[0], 4, 0, EARLY)
    lax.fori_loop(EARLY, SLOTS, to_fourier, 0)
    send(outgoing.at[0], incoming.at[0], 0, EARLY, SLOTS - EARLY)
    send(outgoing.at[1], incoming.at[1], 1)

    table_copies = [
        pltpu.make_async_copy(synthesis_table, synthesis, table_sem.at[0]),
        pltpu.make_async_copy(analysis_table, analysis, table_sem.at[1]),
    ]
    for copy in table_copies:
        copy.start()
    for copy in row_copies:
        copy.wait()

    def build_order(block, carry):
        rows = pl.ds(pl.multiple_of(block * 128, 128), 128)
        number = block * 128 + lax.broadcasted_iota(jnp.int32, (128, 128), 0)
        for place in range(WAVES // 128):
            held = assign_rows[pl.ds(place, 1), :]
            order[rows, pl.ds(place * 128, 128)] = jnp.where(number == held, 1.0, 0.0).astype(BF16)
        return carry

    lax.fori_loop(0, WAVES // 128, build_order, 0)
    for copy in table_copies:
        copy.wait()

    span_lane = lax.broadcasted_iota(jnp.int32, (SPAN, 128), 1)
    left = span_lane < 64
    sign = jnp.where(left, 1.0, -1.0)
    field = lax.rem(span_lane // 8, 4)
    first_row = lax.broadcasted_iota(jnp.int32, (SPAN, 128), 0) == 0

    def cross(value):
        return pltpu.roll(value, 64, 1) + sign * value

    for half in range(2):
        if half == 0:
            settle(outgoing.at[0], incoming.at[0], 4, receive_sem, EARLY)
            own(outgoing.at[0], incoming.at[0], 4, 0, EARLY)
            settle(outgoing.at[0], incoming.at[0], 0, receive_sem, SLOTS - EARLY)
            own(outgoing.at[0], incoming.at[0], 0, EARLY, SLOTS - EARLY)
        else:
            settle(outgoing.at[1], incoming.at[1], 1, receive_sem)
            own(outgoing.at[1], incoming.at[1], 1)
        received = incoming[half]
        received_both = jnp.concatenate(halves(received), axis=1)

        for part in range(PARTS):
            wide = jnp.dot(order[pl.ds(part * SPAN, SPAN), :], received_both, preferred_element_type=F32)
            value = wide[:, :128] + wide[:, 128:]
            waves[part] = jnp.where(first_row, 0.5 * value, value) if part == 0 else value

        for k1 in range(ROUNDS):
            c_sum, s_sum = waves[0], 0.0 * waves[0] if k1 == 0 else 0.0
            for part in range(1, PARTS):
                cosine, sine = turn(k1, part)
                c_sum = c_sum + cosine * waves[part]
                if k1 > 0:
                    s_sum = s_sum + sine * waves[part]
            operand = jnp.concatenate([jnp.where(left, c_sum, -s_sum), jnp.where(left, s_sum, c_sum)], axis=0)
            points = cross(table_product(synthesis[k1], operand))
            other = jnp.where(
                field == 0,
                pltpu.roll(points, 112, 1),
                jnp.where(field == 3, pltpu.roll(points, 16, 1), pltpu.roll(points, 120, 1)),
            )
            terms = points * other
            if k1 == 0:
                terms = jnp.where(left, terms, 0.0)
            found = table_product(analysis[k1], cross(terms))
            even, odd = found[:SPAN], found[SPAN:]
            c_part = jnp.where(left, even, odd)
            s_part = jnp.where(left, odd, -even)
            if k1 == 0:
                for part in range(PARTS):
                    sums[pl.ds(part * SPAN, SPAN), :] = c_part
            else:
                sums[pl.ds(0, SPAN), :] += c_part
                for part in range(1, PARTS):
                    cosine, sine = turn(k1, part)
                    sums[pl.ds(part * SPAN, SPAN), :] += cosine * c_part + sine * s_part

        def to_slots(other):
            for slot in range(SLOTS):
                row = other * SLOTS + slot
                results[half, pl.ds(row, 1), :] = sums[pl.ds(assign_scalar[row], 1), :]

        send(results.at[half], returned.at[half], 2 + half, prepare=to_slots)

    settle(outgoing.at[0], incoming.at[0], 4, send_sem, EARLY)
    settle(outgoing.at[0], incoming.at[0], 0, send_sem, SLOTS - EARLY)
    settle(outgoing.at[1], incoming.at[1], 1, send_sem)
    for half in range(2):
        settle(results.at[half], returned.at[half], 2 + half, receive_sem)
        own(results.at[half], returned.at[half], 2 + half)
        settle(results.at[half], returned.at[half], 2 + half, send_sem)


def harmonic_kernel(assign, function_high, function_low, returned, weights, out, harmonics, store_sem):
    first_number = (lax.axis_index("lat") * 4 + lax.axis_index("wave")) * SLOTS
    even_block = lax.rem(lax.broadcasted_iota(jnp.int32, (PAIRS, 128), 1) // 32, 2) == 0
    scale = weights[...] * (4.0 / POINTS)

    def store_copy(slot):
        return pltpu.make_async_copy(harmonics.at[slot], out.at[slot], store_sem.at[slot])

    def to_harmonics(slot, carry):
        rows = pl.ds(slot, PAIRS, stride=SLOTS)
        first, second = returned[0, rows, :], returned[1, rows, :]
        first_other, second_other = pltpu.roll(first, 96, 1), pltpu.roll(second, 32, 1)
        for parity in range(2):
            if parity == 0:
                folded = jnp.where(even_block, first + first_other, second_other + second)
            else:
                folded = jnp.where(even_block, first - first_other, second_other - second)
            high, low = halves(jnp.transpose(folded) * scale)
            functions = function_high[slot, parity]
            total = jnp.dot(
                jnp.concatenate([high, low], axis=1),
                jnp.concatenate([functions, functions], axis=0),
                preferred_element_type=F32,
            ) + jnp.dot(high, function_low[slot, parity], preferred_element_type=F32)
            total = jnp.where(valid_degrees(assign[first_number + slot], parity, 128), total, 0.0)
            for part in range(2):
                for half in range(2):
                    for field in range(4):
                        source = ((part * 2 + half) * 4 + field) * 8
                        target = ((part * 4 + field) * 2 + half) * 8
                        harmonics[slot, parity, target : target + 8, :] = total[source : source + 8]
        store_copy(slot).start()
        return carry

    lax.fori_loop(0, SLOTS, to_harmonics, 0, unroll=True)
    for slot in range(SLOTS):
        store_copy(slot).wait()


def body(spectra, legendre, weights, counts, assign):
    del counts
    synthesis, analysis = tables()
    any_space = pl.BlockSpec(memory_space=pl.ANY)
    scalar = pl.BlockSpec(memory_space=pltpu.SMEM)
    vector = pl.BlockSpec(memory_space=pltpu.VMEM)
    returned, function_high, function_low = pl.pallas_call(
        grid_kernel,
        out_shape=[
            jax.ShapeDtypeStruct((2, WAVES, 128), F32),
            jax.ShapeDtypeStruct((SLOTS, 2, PAIRS, HALF), BF16),
            jax.ShapeDtypeStruct((SLOTS, 2, PAIRS, HALF), BF16),
        ],
        in_specs=[any_space, any_space, pl.BlockSpec(memory_space=pltpu.HBM), any_space, any_space],
        out_specs=[vector, vector, vector],
        scratch_shapes=[
            pltpu.VMEM((SLOTS, 2, PAIRS, HALF), F32),
            pltpu.VMEM((SLOTS, 2, 2, 2, 4, 8, HALF), F32),
            pltpu.VMEM((ROUNDS, 2 * SPAN, 2 * SPAN), BF16),
            pltpu.VMEM((ROUNDS, 4 * SPAN, SPAN), BF16),
            pltpu.SMEM((WAVES,), jnp.int32),
            pltpu.VMEM((16, 128), jnp.int32),
            pltpu.VMEM((WAVES, WAVES), BF16),
            pltpu.VMEM((2, WAVES, 128), F32),
            pltpu.VMEM((2, WAVES, 128), F32),
            pltpu.VMEM((2, WAVES, 128), F32),
            pltpu.VMEM((PARTS, SPAN, 128), F32),
            pltpu.VMEM((WAVES, 128), F32),
            pltpu.SemaphoreType.DMA((SLOTS, 4)),
            pltpu.SemaphoreType.DMA((3 + WAVES // 128,)),
            pltpu.SemaphoreType.DMA((5,)),
            pltpu.SemaphoreType.DMA((5,)),
            pltpu.SemaphoreType.DMA((5,)),
        ],
        compiler_params=pltpu.CompilerParams(collective_id=0, has_side_effects=True, vmem_limit_bytes=44 << 20),
        name="grid_round_trip",
    )(legendre, spectra.reshape(SLOTS, 2, 2, 4, 2, 8, HALF), assign, jnp.asarray(synthesis), jnp.asarray(analysis))
    return pl.pallas_call(
        harmonic_kernel,
        out_shape=jax.ShapeDtypeStruct((SLOTS, 2, 128, HALF), F32),
        in_specs=[scalar, vector, vector, vector, vector],
        out_specs=any_space,
        scratch_shapes=[pltpu.VMEM((SLOTS, 2, 128, HALF), F32), pltpu.SemaphoreType.DMA((SLOTS,))],
        compiler_params=pltpu.CompilerParams(vmem_limit_bytes=32 << 20),
        name="harmonics",
    )(assign, function_high, function_low, returned, weights.reshape(1, PAIRS))


def solution(mesh):
    placed = (
        P(("lat", "wave"), None, None, None),
        P(None, ("lat", "wave"), None, None),
        P(),
        P("lat"),
        P(),
    )
    return jax.shard_map(
        body,
        mesh=mesh,
        in_specs=placed,
        out_specs=P(("lat", "wave"), None, None, None),
        check_vma=False,
    )
```

```python
import functools
import math

import jax
import jax.numpy as jnp
import ml_dtypes
import numpy as np
from jax import lax
from jax.experimental import pallas as pl
from jax.experimental.pallas import tpu as pltpu
from jax.sharding import PartitionSpec as P

WAVES = 1280
SPAN = 256
RADIX = 15
POINTS = RADIX * SPAN
PARTS = WAVES // SPAN
ROUNDS = RADIX // 2 + 1
SLOTS = 10
EARLY = 6
PAIRS = 128
HALF = 640
DEVICES = 128
OTHERS = DEVICES - 1
MESH = pl.DeviceIdType.MESH
F32 = jnp.float32
BF16 = jnp.bfloat16


def stacked(table):
    high = table.astype(ml_dtypes.bfloat16)
    low = (table - high.astype(np.float64)).astype(ml_dtypes.bfloat16)
    return np.concatenate([high, low], axis=1)


def turn(k1, part):
    angle = 2.0 * math.pi * ((k1 * part) % RADIX) / RADIX
    return math.cos(angle), math.sin(angle)


@functools.cache
def tables():
    k1 = np.arange(ROUNDS)[:, None, None]
    k2 = np.arange(SPAN)[None, :, None]
    m2 = np.arange(SPAN)[None, None, :]
    angle = 2.0 * np.pi * ((m2 * (k1 + RADIX * k2)) % POINTS) / POINTS
    synthesis = np.concatenate([np.cos(angle), -np.sin(angle)], axis=2)
    analysis = np.ascontiguousarray(np.swapaxes(synthesis, 1, 2))
    return stacked(synthesis), stacked(analysis)


def halves(value):
    high = value.astype(BF16)
    low = (value - high.astype(F32)).astype(BF16)
    return high, low


def row_product(high, low, value):
    value_high, value_low = halves(value)
    numbers = (((1,), (1,)), ((), ()))
    both = jnp.concatenate([value_high, value_low], axis=0)
    width = value.shape[0]
    wide = lax.dot_general(high, both, numbers, preferred_element_type=F32)
    total = wide[:, :width] + wide[:, width:]
    return total + lax.dot_general(low, value_high, numbers, preferred_element_type=F32)


def table_product(table, value):
    wide = jnp.dot(table, jnp.concatenate(halves(value), axis=1), preferred_element_type=F32)
    rows, width = wide.shape[0] // 2, value.shape[1]
    return wide[:rows, :width] + (wide[:rows, width:] + wide[rows:, :width])


def for_others(lat, wave, act):
    z, y, core = lat // 8, lax.rem(lat // 2, 4), lax.rem(lat, 2)
    cores = [core, 1 - core]
    xs = [lax.rem(wave + offset, 4) for offset in range(4)]

    def group(step, carry, places=range(8)):
        z_step, y_step = z + step // 4, y + lax.rem(step, 4)
        for place in places:
            other_z, other_y = lax.rem(z_step + place, 4), lax.rem(y_step + place // 2, 4)
            act(other_z * 8 + other_y * 2 + cores[place // 4], xs[place % 4])
        return carry

    group(0, 0, range(1, 8))
    lax.fori_loop(1, 16, group, 0)


def valid_degrees(number, parity, rows):
    degree = 2 * lax.broadcasted_iota(jnp.int32, (rows, HALF), 1) + parity
    return degree < WAVES - number


def grid_kernel(
    legendre, spectra, assign, synthesis_table, analysis_table,
    returned, function_high, function_low,
    functions, coefficients, synthesis, analysis, assign_scalar, assign_rows, order,
    outgoing, incoming, results, waves, sums, load_sem, table_sem, send_sem, receive_sem, own_sem,
):
    lat, wave = lax.axis_index("lat"), lax.axis_index("wave")
    me = lat * 4 + wave
    barrier = pltpu.get_barrier_semaphore()

    def function_copy(slot, parity):
        return pltpu.make_async_copy(legendre.at[:, slot, parity], functions.at[slot, parity], load_sem.at[slot, parity])

    def coefficient_copy(slot, half):
        return pltpu.make_async_copy(
            spectra.at[slot, :, :, :, half], coefficients.at[slot, :, :, half], load_sem.at[slot, 2 + half]
        )

    scalar_copy = pltpu.make_async_copy(assign, assign_scalar, table_sem.at[2 + WAVES // 128])
    scalar_copy.start()

    def start_loads(slot, carry):
        for place in range(2):
            coefficient_copy(slot, place).start()
            function_copy(slot, place).start()
        return carry

    lax.fori_loop(0, 2, start_loads, 0)
    def greet(other_lat, other_wave):
        pl.semaphore_signal(barrier, inc=1, device_id=(other_lat, other_wave), device_id_type=MESH)

    for_others(lat, wave, greet)
    lax.fori_loop(2, SLOTS, start_loads, 0)
    row_copies = [
        pltpu.make_async_copy(assign.at[pl.ds(row * 128, 128)], assign_rows.at[row], table_sem.at[2 + row])
        for row in range(WAVES // 128)
    ]
    for copy in row_copies:
        copy.start()


    lane = lax.broadcasted_iota(jnp.int32, (PAIRS, 128), 1)
    even_block = lax.rem(lane // 32, 2) == 0

    def to_fourier(slot, carry):
        for place in range(2):
            coefficient_copy(slot, place).wait()
            function_copy(slot, place).wait()
        number = assign_scalar[me * SLOTS + slot]
        parts = []
        for parity in range(2):
            values = coefficients[slot, parity].reshape(128, HALF)
            masked = jnp.where(valid_degrees(number, parity, 128), values, 0.0)
            high, low = halves(functions[slot, parity])
            function_high[slot, parity] = high
            function_low[slot, parity] = low
            parts.append(row_product(high, low, masked))
        north, south = parts[0] + parts[1], parts[0] - parts[1]
        rows = pl.ds(slot, PAIRS, stride=SLOTS)
        outgoing[0, rows, :] = jnp.where(even_block, north, pltpu.roll(south, 32, 1))
        outgoing[1, rows, :] = jnp.where(even_block, pltpu.roll(north, 96, 1), south)
        return carry

    def send(source, target, place, first=0, count=SLOTS, prepare=None):
        def one(other_lat, other_wave):
            other = other_lat * 4 + other_wave
            if prepare is not None:
                prepare(other)
            pltpu.make_async_remote_copy(
                source.at[pl.ds(other * SLOTS + first, count)],
                target.at[pl.ds(me * SLOTS + first, count)],
                send_sem.at[place],
                receive_sem.at[place],
                device_id=(other_lat, other_wave),
                device_id_type=MESH,
            ).start()

        for_others(lat, wave, one)
        if prepare is not None:
            prepare(me)
        mine = pl.ds(me * SLOTS + first, count)
        pltpu.make_async_copy(source.at[mine], target.at[mine], own_sem.at[place]).start()

    def settle(source, target, place, sem, count=SLOTS):
        rows = pl.ds(0, OTHERS * count)
        pltpu.make_async_copy(source.at[rows], target.at[rows], sem.at[place]).wait()

    def own(source, target, place, first=0, count=SLOTS):
        mine = pl.ds(me * SLOTS + first, count)
        pltpu.make_async_copy(source.at[mine], target.at[mine], own_sem.at[place]).wait()

    scalar_copy.wait()
    lax.fori_loop(0, EARLY, to_fourier, 0, unroll=True)
    pl.semaphore_wait(barrier, OTHERS)
    send(outgoing.at[0], incoming.at[0], 4, 0, EARLY)
    lax.fori_loop(EARLY, SLOTS, to_fourier, 0, unroll=True)
    send(outgoing.at[0], incoming.at[0], 0, EARLY, SLOTS - EARLY)
    send(outgoing.at[1], incoming.at[1], 1)

    table_copies = [
        pltpu.make_async_copy(synthesis_table, synthesis, table_sem.at[0]),
        pltpu.make_async_copy(analysis_table, analysis, table_sem.at[1]),
    ]
    for copy in table_copies:
        copy.start()
    for copy in row_copies:
        copy.wait()

    def build_order(block, carry):
        rows = pl.ds(pl.multiple_of(block * 128, 128), 128)
        number = block * 128 + lax.broadcasted_iota(jnp.int32, (128, 128), 0)
        for place in range(WAVES // 128):
            held = assign_rows[pl.ds(place, 1), :]
            order[rows, pl.ds(place * 128, 128)] = jnp.where(number == held, 1.0, 0.0).astype(BF16)
        return carry

    lax.fori_loop(0, WAVES // 128, build_order, 0)
    for copy in table_copies:
        copy.wait()

    span_lane = lax.broadcasted_iota(jnp.int32, (SPAN, 128), 1)
    left = span_lane < 64
    sign = jnp.where(left, 1.0, -1.0)
    field = lax.rem(span_lane // 8, 4)
    first_row = lax.broadcasted_iota(jnp.int32, (SPAN, 128), 0) == 0

    def cross(value):
        return pltpu.roll(value, 64, 1) + sign * value

    for half in range(2):
        if half == 0:
            settle(outgoing.at[0], incoming.at[0], 4, receive_sem, EARLY)
            own(outgoing.at[0], incoming.at[0], 4, 0, EARLY)
            settle(outgoing.at[0], incoming.at[0], 0, receive_sem, SLOTS - EARLY)
            own(outgoing.at[0], incoming.at[0], 0, EARLY, SLOTS - EARLY)
        else:
            settle(outgoing.at[1], incoming.at[1], 1, receive_sem)
            own(outgoing.at[1], incoming.at[1], 1)
        received = incoming[half]
        received_both = jnp.concatenate(halves(received), axis=1)

        for part in range(PARTS):
            wide = jnp.dot(order[pl.ds(part * SPAN, SPAN), :], received_both, preferred_element_type=F32)
            value = wide[:, :128] + wide[:, 128:]
            waves[part] = jnp.where(first_row, 0.5 * value, value) if part == 0 else value

        for k1 in range(ROUNDS):
            c_sum, s_sum = waves[0], 0.0 * waves[0] if k1 == 0 else 0.0
            for part in range(1, PARTS):
                cosine, sine = turn(k1, part)
                c_sum = c_sum + cosine * waves[part]
                if k1 > 0:
                    s_sum = s_sum + sine * waves[part]
            operand = jnp.concatenate([jnp.where(left, c_sum, -s_sum), jnp.where(left, s_sum, c_sum)], axis=0)
            points = cross(table_product(synthesis[k1], operand))
            other = jnp.where(
                field == 0,
                pltpu.roll(points, 112, 1),
                jnp.where(field == 3, pltpu.roll(points, 16, 1), pltpu.roll(points, 120, 1)),
            )
            terms = points * other
            if k1 == 0:
                terms = jnp.where(left, terms, 0.0)
            found = table_product(analysis[k1], cross(terms))
            even, odd = found[:SPAN], found[SPAN:]
            c_part = jnp.where(left, even, odd)
            s_part = jnp.where(left, odd, -even)
            if k1 == 0:
                for part in range(PARTS):
                    sums[pl.ds(part * SPAN, SPAN), :] = c_part
            else:
                sums[pl.ds(0, SPAN), :] += c_part
                for part in range(1, PARTS):
                    cosine, sine = turn(k1, part)
                    sums[pl.ds(part * SPAN, SPAN), :] += cosine * c_part + sine * s_part

        def to_slots(other):
            for slot in range(SLOTS):
                row = other * SLOTS + slot
                results[half, pl.ds(row, 1), :] = sums[pl.ds(assign_scalar[row], 1), :]

        send(results.at[half], returned.at[half], 2 + half, prepare=to_slots)

    settle(outgoing.at[0], incoming.at[0], 4, send_sem, EARLY)
    settle(outgoing.at[0], incoming.at[0], 0, send_sem, SLOTS - EARLY)
    settle(outgoing.at[1], incoming.at[1], 1, send_sem)
    for half in range(2):
        settle(results.at[half], returned.at[half], 2 + half, receive_sem)
        own(results.at[half], returned.at[half], 2 + half)
        settle(results.at[half], returned.at[half], 2 + half, send_sem)


def harmonic_kernel(assign, function_high, function_low, returned, weights, out, harmonics, store_sem):
    first_number = (lax.axis_index("lat") * 4 + lax.axis_index("wave")) * SLOTS
    even_block = lax.rem(lax.broadcasted_iota(jnp.int32, (PAIRS, 128), 1) // 32, 2) == 0
    scale = weights[...] * (4.0 / POINTS)

    def store_copy(slot):
        return pltpu.make_async_copy(harmonics.at[slot], out.at[slot], store_sem.at[slot])

    def to_harmonics(slot, carry):
        rows = pl.ds(slot, PAIRS, stride=SLOTS)
        first, second = returned[0, rows, :], returned[1, rows, :]
        first_other, second_other = pltpu.roll(first, 96, 1), pltpu.roll(second, 32, 1)
        for parity in range(2):
            if parity == 0:
                folded = jnp.where(even_block, first + first_other, second_other + second)
            else:
                folded = jnp.where(even_block, first - first_other, second_other - second)
            high, low = halves(jnp.transpose(folded) * scale)
            functions = function_high[slot, parity]
            total = jnp.dot(
                jnp.concatenate([high, low], axis=1),
                jnp.concatenate([functions, functions], axis=0),
                preferred_element_type=F32,
            ) + jnp.dot(high, function_low[slot, parity], preferred_element_type=F32)
            total = jnp.where(valid_degrees(assign[first_number + slot], parity, 128), total, 0.0)
            for part in range(2):
                for half in range(2):
                    for field in range(4):
                        source = ((part * 2 + half) * 4 + field) * 8
                        target = ((part * 4 + field) * 2 + half) * 8
                        harmonics[slot, parity, target : target + 8, :] = total[source : source + 8]
        store_copy(slot).start()
        return carry

    lax.fori_loop(0, SLOTS, to_harmonics, 0, unroll=True)
    for slot in range(SLOTS):
        store_copy(slot).wait()


def body(spectra, legendre, weights, counts, assign):
    del counts
    synthesis, analysis = tables()
    any_space = pl.BlockSpec(memory_space=pl.ANY)
    scalar = pl.BlockSpec(memory_space=pltpu.SMEM)
    vector = pl.BlockSpec(memory_space=pltpu.VMEM)
    returned, function_high, function_low = pl.pallas_call(
        grid_kernel,
        out_shape=[
            jax.ShapeDtypeStruct((2, WAVES, 128), F32),
            jax.ShapeDtypeStruct((SLOTS, 2, PAIRS, HALF), BF16),
            jax.ShapeDtypeStruct((SLOTS, 2, PAIRS, HALF), BF16),
        ],
        in_specs=[any_space, any_space, pl.BlockSpec(memory_space=pltpu.HBM), any_space, any_space],
        out_specs=[vector, vector, vector],
        scratch_shapes=[
            pltpu.VMEM((SLOTS, 2, PAIRS, HALF), F32),
            pltpu.VMEM((SLOTS, 2, 2, 2, 4, 8, HALF), F32),
            pltpu.VMEM((ROUNDS, 2 * SPAN, 2 * SPAN), BF16),
            pltpu.VMEM((ROUNDS, 4 * SPAN, SPAN), BF16),
            pltpu.SMEM((WAVES,), jnp.int32),
            pltpu.VMEM((16, 128), jnp.int32),
            pltpu.VMEM((WAVES, WAVES), BF16),
            pltpu.VMEM((2, WAVES, 128), F32),
            pltpu.VMEM((2, WAVES, 128), F32),
            pltpu.VMEM((2, WAVES, 128), F32),
            pltpu.VMEM((PARTS, SPAN, 128), F32),
            pltpu.VMEM((WAVES, 128), F32),
            pltpu.SemaphoreType.DMA((SLOTS, 4)),
            pltpu.SemaphoreType.DMA((3 + WAVES // 128,)),
            pltpu.SemaphoreType.DMA((5,)),
            pltpu.SemaphoreType.DMA((5,)),
            pltpu.SemaphoreType.DMA((5,)),
        ],
        compiler_params=pltpu.CompilerParams(collective_id=0, has_side_effects=True, vmem_limit_bytes=44 << 20),
        name="grid_round_trip",
    )(legendre, spectra.reshape(SLOTS, 2, 2, 4, 2, 8, HALF), assign, jnp.asarray(synthesis), jnp.asarray(analysis))
    return pl.pallas_call(
        harmonic_kernel,
        out_shape=jax.ShapeDtypeStruct((SLOTS, 2, 128, HALF), F32),
        in_specs=[scalar, vector, vector, vector, vector],
        out_specs=any_space,
        scratch_shapes=[pltpu.VMEM((SLOTS, 2, 128, HALF), F32), pltpu.SemaphoreType.DMA((SLOTS,))],
        compiler_params=pltpu.CompilerParams(vmem_limit_bytes=32 << 20),
        name="harmonics",
    )(assign, function_high, function_low, returned, weights.reshape(1, PAIRS))


def solution(mesh):
    placed = (
        P(("lat", "wave"), None, None, None),
        P(None, ("lat", "wave"), None, None),
        P(),
        P("lat"),
        P(),
    )
    return jax.shard_map(
        body,
        mesh=mesh,
        in_specs=placed,
        out_specs=P(("lat", "wave"), None, None, None),
        check_vma=False,
    )
```

```python
import functools
import math

import jax
import jax.numpy as jnp
import ml_dtypes
import numpy as np
from jax import lax
from jax.experimental import pallas as pl
from jax.experimental.pallas import tpu as pltpu
from jax.sharding import PartitionSpec as P

WAVES = 1280
SPAN = 256
RADIX = 15
POINTS = RADIX * SPAN
PARTS = WAVES // SPAN
ROUNDS = RADIX // 2 + 1
SLOTS = 10
EARLY = 6
PAIRS = 128
HALF = 640
DEVICES = 128
OTHERS = DEVICES - 1
MESH = pl.DeviceIdType.MESH
F32 = jnp.float32
BF16 = jnp.bfloat16


def stacked(table):
    high = table.astype(ml_dtypes.bfloat16)
    low = (table - high.astype(np.float64)).astype(ml_dtypes.bfloat16)
    return np.concatenate([high, low], axis=1)


def turn(k1, part):
    angle = 2.0 * math.pi * ((k1 * part) % RADIX) / RADIX
    return math.cos(angle), math.sin(angle)


@functools.cache
def tables():
    k1 = np.arange(ROUNDS)[:, None, None]
    k2 = np.arange(SPAN)[None, :, None]
    m2 = np.arange(SPAN)[None, None, :]
    angle = 2.0 * np.pi * ((m2 * (k1 + RADIX * k2)) % POINTS) / POINTS
    synthesis = np.concatenate([np.cos(angle), -np.sin(angle)], axis=2)
    analysis = np.ascontiguousarray(np.swapaxes(synthesis, 1, 2))
    return stacked(synthesis), stacked(analysis)


def halves(value):
    high = value.astype(BF16)
    low = (value - high.astype(F32)).astype(BF16)
    return high, low


def row_product(high, low, value):
    value_high, value_low = halves(value)
    numbers = (((1,), (1,)), ((), ()))
    both = jnp.concatenate([value_high, value_low], axis=0)
    width = value.shape[0]
    wide = lax.dot_general(high, both, numbers, preferred_element_type=F32)
    total = wide[:, :width] + wide[:, width:]
    return total + lax.dot_general(low, value_high, numbers, preferred_element_type=F32)


def table_product(table, value):
    wide = jnp.dot(table, jnp.concatenate(halves(value), axis=1), preferred_element_type=F32)
    rows, width = wide.shape[0] // 2, value.shape[1]
    return wide[:rows, :width] + (wide[:rows, width:] + wide[rows:, :width])


def for_others(lat, wave, act, unroll=1):
    z, y, core = lat // 8, lax.rem(lat // 2, 4), lax.rem(lat, 2)
    cores = [core, 1 - core]
    xs = [lax.rem(wave + offset, 4) for offset in range(4)]

    def group(step, carry, places=range(8)):
        z_step, y_step = z + step // 4, y + lax.rem(step, 4)
        for place in places:
            other_z, other_y = lax.rem(z_step + place, 4), lax.rem(y_step + place // 2, 4)
            act(other_z * 8 + other_y * 2 + cores[place // 4], xs[place % 4])
        return carry

    group(0, 0, range(1, 8))
    lax.fori_loop(1, 16, group, 0, unroll=unroll)


def valid_degrees(number, parity, rows):
    degree = 2 * lax.broadcasted_iota(jnp.int32, (rows, HALF), 1) + parity
    return degree < WAVES - number


def grid_kernel(
    legendre, spectra, assign, synthesis_table, analysis_table,
    returned, function_high, function_low,
    functions, coefficients, synthesis, analysis, assign_scalar, assign_rows, order,
    outgoing, incoming, results, waves, sums, load_sem, table_sem, send_sem, receive_sem, own_sem,
):
    lat, wave = lax.axis_index("lat"), lax.axis_index("wave")
    me = lat * 4 + wave
    barrier = pltpu.get_barrier_semaphore()

    def function_copy(slot, parity):
        return pltpu.make_async_copy(legendre.at[:, slot, parity], functions.at[slot, parity], load_sem.at[slot, parity])

    def coefficient_copy(slot, half):
        return pltpu.make_async_copy(
            spectra.at[slot, :, :, :, half], coefficients.at[slot, :, :, half], load_sem.at[slot, 2 + half]
        )

    scalar_copy = pltpu.make_async_copy(assign, assign_scalar, table_sem.at[2 + WAVES // 128])
    scalar_copy.start()

    def start_loads(slot, carry):
        for place in range(2):
            coefficient_copy(slot, place).start()
            function_copy(slot, place).start()
        return carry

    lax.fori_loop(0, 2, start_loads, 0)
    def greet(other_lat, other_wave):
        pl.semaphore_signal(barrier, inc=1, device_id=(other_lat, other_wave), device_id_type=MESH)

    for_others(lat, wave, greet)
    lax.fori_loop(2, SLOTS, start_loads, 0)
    row_copies = [
        pltpu.make_async_copy(assign.at[pl.ds(row * 128, 128)], assign_rows.at[row], table_sem.at[2 + row])
        for row in range(WAVES // 128)
    ]
    for copy in row_copies:
        copy.start()


    lane = lax.broadcasted_iota(jnp.int32, (PAIRS, 128), 1)
    even_block = lax.rem(lane // 32, 2) == 0

    def to_fourier(slot, carry):
        for place in range(2):
            coefficient_copy(slot, place).wait()
            function_copy(slot, place).wait()
        number = assign_scalar[me * SLOTS + slot]
        parts = []
        for parity in range(2):
            values = coefficients[slot, parity].reshape(128, HALF)
            masked = jnp.where(valid_degrees(number, parity, 128), values, 0.0)
            high, low = halves(functions[slot, parity])
            function_high[slot, parity] = high
            function_low[slot, parity] = low
            parts.append(row_product(high, low, masked))
        north, south = parts[0] + parts[1], parts[0] - parts[1]
        rows = pl.ds(slot, PAIRS, stride=SLOTS)
        outgoing[0, rows, :] = jnp.where(even_block, north, pltpu.roll(south, 32, 1))
        outgoing[1, rows, :] = jnp.where(even_block, pltpu.roll(north, 96, 1), south)
        return carry

    def send(source, target, place, first=0, count=SLOTS, prepare=None):
        def one(other_lat, other_wave):
            other = other_lat * 4 + other_wave
            if prepare is not None:
                prepare(other)
            pltpu.make_async_remote_copy(
                source.at[pl.ds(other * SLOTS + first, count)],
                target.at[pl.ds(me * SLOTS + first, count)],
                send_sem.at[place],
                receive_sem.at[place],
                device_id=(other_lat, other_wave),
                device_id_type=MESH,
            ).start()

        for_others(lat, wave, one, 1 if prepare is None else 3)
        if prepare is not None:
            prepare(me)
        mine = pl.ds(me * SLOTS + first, count)
        pltpu.make_async_copy(source.at[mine], target.at[mine], own_sem.at[place]).start()

    def settle(source, target, place, sem, count=SLOTS):
        rows = pl.ds(0, OTHERS * count)
        pltpu.make_async_copy(source.at[rows], target.at[rows], sem.at[place]).wait()

    def own(source, target, place, first=0, count=SLOTS):
        mine = pl.ds(me * SLOTS + first, count)
        pltpu.make_async_copy(source.at[mine], target.at[mine], own_sem.at[place]).wait()

    scalar_copy.wait()
    lax.fori_loop(0, EARLY, to_fourier, 0, unroll=True)
    pl.semaphore_wait(barrier, OTHERS)
    send(outgoing.at[0], incoming.at[0], 4, 0, EARLY)
    lax.fori_loop(EARLY, SLOTS, to_fourier, 0, unroll=True)
    send(outgoing.at[0], incoming.at[0], 0, EARLY, SLOTS - EARLY)
    send(outgoing.at[1], incoming.at[1], 1)

    table_copies = [
        pltpu.make_async_copy(synthesis_table, synthesis, table_sem.at[0]),
        pltpu.make_async_copy(analysis_table, analysis, table_sem.at[1]),
    ]
    for copy in table_copies:
        copy.start()
    for copy in row_copies:
        copy.wait()

    def build_order(block, carry):
        rows = pl.ds(pl.multiple_of(block * 128, 128), 128)
        number = block * 128 + lax.broadcasted_iota(jnp.int32, (128, 128), 0)
        for place in range(WAVES // 128):
            held = assign_rows[pl.ds(place, 1), :]
            order[rows, pl.ds(place * 128, 128)] = jnp.where(number == held, 1.0, 0.0).astype(BF16)
        return carry

    lax.fori_loop(0, WAVES // 128, build_order, 0)
    for copy in table_copies:
        copy.wait()

    span_lane = lax.broadcasted_iota(jnp.int32, (SPAN, 128), 1)
    left = span_lane < 64
    sign = jnp.where(left, 1.0, -1.0)
    field = lax.rem(span_lane // 8, 4)
    first_row = lax.broadcasted_iota(jnp.int32, (SPAN, 128), 0) == 0

    def cross(value):
        return pltpu.roll(value, 64, 1) + sign * value

    for half in range(2):
        if half == 0:
            settle(outgoing.at[0], incoming.at[0], 4, receive_sem, EARLY)
            own(outgoing.at[0], incoming.at[0], 4, 0, EARLY)
            settle(outgoing.at[0], incoming.at[0], 0, receive_sem, SLOTS - EARLY)
            own(outgoing.at[0], incoming.at[0], 0, EARLY, SLOTS - EARLY)
        else:
            settle(outgoing.at[1], incoming.at[1], 1, receive_sem)
            own(outgoing.at[1], incoming.at[1], 1)
        received = incoming[half]
        received_both = jnp.concatenate(halves(received), axis=1)

        wide = jnp.dot(order[...], received_both, preferred_element_type=F32)
        for part in range(PARTS):
            block = wide[part * SPAN : (part + 1) * SPAN]
            value = block[:, :128] + block[:, 128:]
            waves[part] = jnp.where(first_row, 0.5 * value, value) if part == 0 else value

        for k1 in range(ROUNDS):
            c_sum, s_sum = waves[0], 0.0 * waves[0] if k1 == 0 else 0.0
            for part in range(1, PARTS):
                cosine, sine = turn(k1, part)
                c_sum = c_sum + cosine * waves[part]
                if k1 > 0:
                    s_sum = s_sum + sine * waves[part]
            operand = jnp.concatenate([jnp.where(left, c_sum, -s_sum), jnp.where(left, s_sum, c_sum)], axis=0)
            points = cross(table_product(synthesis[k1], operand))
            other = jnp.where(
                field == 0,
                pltpu.roll(points, 112, 1),
                jnp.where(field == 3, pltpu.roll(points, 16, 1), pltpu.roll(points, 120, 1)),
            )
            terms = points * other
            if k1 == 0:
                terms = jnp.where(left, terms, 0.0)
            found = table_product(analysis[k1], cross(terms))
            even, odd = found[:SPAN], found[SPAN:]
            c_part = jnp.where(left, even, odd)
            s_part = jnp.where(left, odd, -even)
            if k1 == 0:
                for part in range(PARTS):
                    sums[pl.ds(part * SPAN, SPAN), :] = c_part
            else:
                sums[pl.ds(0, SPAN), :] += c_part
                for part in range(1, PARTS):
                    cosine, sine = turn(k1, part)
                    sums[pl.ds(part * SPAN, SPAN), :] += cosine * c_part + sine * s_part

        def to_slots(other):
            for slot in range(SLOTS):
                row = other * SLOTS + slot
                results[half, pl.ds(row, 1), :] = sums[pl.ds(assign_scalar[row], 1), :]

        send(results.at[half], returned.at[half], 2 + half, prepare=to_slots)

    settle(outgoing.at[0], incoming.at[0], 4, send_sem, EARLY)
    settle(outgoing.at[0], incoming.at[0], 0, send_sem, SLOTS - EARLY)
    settle(outgoing.at[1], incoming.at[1], 1, send_sem)
    for half in range(2):
        settle(results.at[half], returned.at[half], 2 + half, receive_sem)
        own(results.at[half], returned.at[half], 2 + half)
        settle(results.at[half], returned.at[half], 2 + half, send_sem)


def harmonic_kernel(assign, function_high, function_low, returned, weights, out, harmonics, store_sem):
    first_number = (lax.axis_index("lat") * 4 + lax.axis_index("wave")) * SLOTS
    even_block = lax.rem(lax.broadcasted_iota(jnp.int32, (PAIRS, 128), 1) // 32, 2) == 0
    scale = weights[...] * (4.0 / POINTS)

    def store_copy(slot):
        return pltpu.make_async_copy(harmonics.at[slot], out.at[slot], store_sem.at[slot])

    def to_harmonics(slot, carry):
        rows = pl.ds(slot, PAIRS, stride=SLOTS)
        first, second = returned[0, rows, :], returned[1, rows, :]
        first_other, second_other = pltpu.roll(first, 96, 1), pltpu.roll(second, 32, 1)
        for parity in range(2):
            if parity == 0:
                folded = jnp.where(even_block, first + first_other, second_other + second)
            else:
                folded = jnp.where(even_block, first - first_other, second_other - second)
            high, low = halves(jnp.transpose(folded) * scale)
            functions = function_high[slot, parity]
            total = jnp.dot(
                jnp.concatenate([high, low], axis=1),
                jnp.concatenate([functions, functions], axis=0),
                preferred_element_type=F32,
            ) + jnp.dot(high, function_low[slot, parity], preferred_element_type=F32)
            total = jnp.where(valid_degrees(assign[first_number + slot], parity, 128), total, 0.0)
            for part in range(2):
                for half in range(2):
                    for field in range(4):
                        source = ((part * 2 + half) * 4 + field) * 8
                        target = ((part * 4 + field) * 2 + half) * 8
                        harmonics[slot, parity, target : target + 8, :] = total[source : source + 8]
        store_copy(slot).start()
        return carry

    lax.fori_loop(0, SLOTS, to_harmonics, 0, unroll=True)
    for slot in range(SLOTS):
        store_copy(slot).wait()


def body(spectra, legendre, weights, counts, assign):
    del counts
    synthesis, analysis = tables()
    any_space = pl.BlockSpec(memory_space=pl.ANY)
    scalar = pl.BlockSpec(memory_space=pltpu.SMEM)
    vector = pl.BlockSpec(memory_space=pltpu.VMEM)
    returned, function_high, function_low = pl.pallas_call(
        grid_kernel,
        out_shape=[
            jax.ShapeDtypeStruct((2, WAVES, 128), F32),
            jax.ShapeDtypeStruct((SLOTS, 2, PAIRS, HALF), BF16),
            jax.ShapeDtypeStruct((SLOTS, 2, PAIRS, HALF), BF16),
        ],
        in_specs=[any_space, any_space, pl.BlockSpec(memory_space=pltpu.HBM), any_space, any_space],
        out_specs=[vector, vector, vector],
        scratch_shapes=[
            pltpu.VMEM((SLOTS, 2, PAIRS, HALF), F32),
            pltpu.VMEM((SLOTS, 2, 2, 2, 4, 8, HALF), F32),
            pltpu.VMEM((ROUNDS, 2 * SPAN, 2 * SPAN), BF16),
            pltpu.VMEM((ROUNDS, 4 * SPAN, SPAN), BF16),
            pltpu.SMEM((WAVES,), jnp.int32),
            pltpu.VMEM((16, 128), jnp.int32),
            pltpu.VMEM((WAVES, WAVES), BF16),
            pltpu.VMEM((2, WAVES, 128), F32),
            pltpu.VMEM((2, WAVES, 128), F32),
            pltpu.VMEM((2, WAVES, 128), F32),
            pltpu.VMEM((PARTS, SPAN, 128), F32),
            pltpu.VMEM((WAVES, 128), F32),
            pltpu.SemaphoreType.DMA((SLOTS, 4)),
            pltpu.SemaphoreType.DMA((3 + WAVES // 128,)),
            pltpu.SemaphoreType.DMA((5,)),
            pltpu.SemaphoreType.DMA((5,)),
            pltpu.SemaphoreType.DMA((5,)),
        ],
        compiler_params=pltpu.CompilerParams(collective_id=0, has_side_effects=True, vmem_limit_bytes=44 << 20),
        name="grid_round_trip",
    )(legendre, spectra.reshape(SLOTS, 2, 2, 4, 2, 8, HALF), assign, jnp.asarray(synthesis), jnp.asarray(analysis))
    return pl.pallas_call(
        harmonic_kernel,
        out_shape=jax.ShapeDtypeStruct((SLOTS, 2, 128, HALF), F32),
        in_specs=[scalar, vector, vector, vector, vector],
        out_specs=any_space,
        scratch_shapes=[pltpu.VMEM((SLOTS, 2, 128, HALF), F32), pltpu.SemaphoreType.DMA((SLOTS,))],
        compiler_params=pltpu.CompilerParams(vmem_limit_bytes=32 << 20),
        name="harmonics",
    )(assign, function_high, function_low, returned, weights.reshape(1, PAIRS))


def solution(mesh):
    placed = (
        P(("lat", "wave"), None, None, None),
        P(None, ("lat", "wave"), None, None),
        P(),
        P("lat"),
        P(),
    )
    return jax.shard_map(
        body,
        mesh=mesh,
        in_specs=placed,
        out_specs=P(("lat", "wave"), None, None, None),
        check_vma=False,
    )
```
